32 devices in a mesh: slab: 16 (over z, y, x), batch: 2 (over core).
Axes of the slice: x: 2, y: 2, z: 4, core: 2. Of those that a mesh axis runs over, the one named last changes fastest.
Arguments:
- query_rows: bfloat16 [1792, 1536], P(('batch', 'slab')), parts along dimension 0, may hold values from -48 to 48
- key_rows: bfloat16 [1792, 1536], P(('batch', 'slab')), parts along dimension 0, may hold values from -6 to 6
- value_rows: bfloat16 [1792, 1536], P(('batch', 'slab')), parts along dimension 0, may hold values from -6 to 6
Outputs:
- attended: bfloat16 [1792, 1536], P(('batch', 'slab')), parts along dimension 0
The draws below stay inside these ranges and needn't reach their ends.
There are 2 independent parts, one for each index of `batch`. The reference program is written for one: setup_inputs(seed, part) draws one part's arguments, and reference() takes and returns one part's arrays. A program takes and returns all parts, laid end to end along the dimension named above; each array names one. Nothing has to cross between parts.
All inputs are finite; a program needn't handle non-finite values.
Results may differ from the reference program's by a relative error of at most 0.005.
Values may be sent and summed in bfloat16 or wider, within the bound.
No kernel may reach another device: no remote copies, remote signals or barrier semaphores. Data moves between devices by JAX's collectives and lax.ppermute only.
A program may use at most 64 MiB of HBM per device.

```python
import math
import jax
import jax.numpy as jnp
from jax import lax

HEADS = 24
HEAD_DIM = 64
TOKENS = 896


def shared_keys(key):
    width = HEADS * HEAD_DIM
    base = jax.random.fold_in(key, 11)
    drawn = jnp.clip(jax.random.normal(base, (TOKENS, width), jnp.float32), -6.0, 6.0)
    return drawn


def draw_key_rows(key, part):
    drawn = shared_keys(key)
    return drawn.astype(jnp.bfloat16)


def draw_query_rows(key, part):
    width = HEADS * HEAD_DIM
    base = jax.random.fold_in(key, 21)
    drawn = jnp.clip(2.5 * jax.random.normal(base, (TOKENS, width), jnp.float32), -15.0, 15.0)
    return drawn.astype(jnp.bfloat16)


def steps_of(own_key, dims, split, least, high):
    factor_of = 1.0
    for position, blocks in split:
        steps = jax.random.uniform(jax.random.fold_in(jax.random.fold_in(own_key, 6), position), (blocks,), jnp.float32, least / len(split), high / len(split))
        factor_of = factor_of * jnp.repeat(jnp.exp(steps), dims[position] // blocks).reshape((-1,) + (1,) * (len(dims) - 1 - position))
    return factor_of


def normal_values(rng, shape, spread, limit, shards=(), dtype=jnp.bfloat16):
    factor_of = steps_of(rng, shape, shards, -0.22, 0.18) if shards else 1.0
    entries = jax.random.normal(rng, shape, jnp.float32) * spread * factor_of
    return jnp.minimum(jnp.maximum(entries, -limit), limit).astype(dtype)


def setup_inputs(seed: int = 0, part: int = 0) -> dict:
    seeds = jax.random.split(jax.random.key(seed), 4)
    part_keys = jax.random.split(jax.random.fold_in(seeds[3], part), 4)
    query_rows = draw_query_rows(jax.random.fold_in(jax.random.fold_in(seeds[3], part), 71), part)
    key_rows = draw_key_rows(jax.random.fold_in(jax.random.fold_in(seeds[3], part), 71), part)
    value_rows = normal_values(part_keys[2], (TOKENS, HEADS * HEAD_DIM), 1.0, 6.0, ((0, 16),))
    return {"query_rows": query_rows, "key_rows": key_rows, "value_rows": value_rows}


def reference(query_rows, key_rows, value_rows):
    count = query_rows.shape[0]
    width = query_rows.shape[1]
    heads = width // HEAD_DIM
    scale = HEAD_DIM ** -0.5
    keys_all = key_rows.astype(jnp.float32).reshape(count, heads, HEAD_DIM)
    values_all = value_rows.astype(jnp.float32).reshape(count, heads, HEAD_DIM)
    block = math.gcd(count, 256)
    queries = query_rows.reshape(count // block, block, heads, HEAD_DIM)

    def one_block(query_block):
        scores = jnp.einsum("qhd,khd->qhk", query_block.astype(jnp.float32), keys_all) * scale
        row_max = jnp.max(scores, axis=-1, keepdims=True)
        expo = jnp.exp(scores - row_max)
        total = jnp.sum(expo, axis=-1)
        weights = expo.astype(jnp.bfloat16).astype(jnp.float32)
        mixed = jnp.einsum("qhk,khd->qhd", weights, values_all)
        return (mixed / total[..., None]).reshape(block, width).astype(jnp.bfloat16)

    return lax.map(one_block, queries).reshape(count, width)
```

```python
import jax
import jax.numpy as jnp
from jax import lax
from jax.experimental import pallas as pl
from jax.experimental.pallas import tpu as pltpu
from jax.sharding import PartitionSpec as P

HEAD_DIM = 64
PAIR = 2 * HEAD_DIM
TRIPLE = 3 * HEAD_DIM
LOG2E = 1.4426950408889634


def window(owner):
    return (owner // 2) * TRIPLE + (owner % 2) * HEAD_DIM


def pack_kernel(owners, q_ref, k_ref, v_ref, out_ref):
    for owner in range(owners):
        start = window(owner)
        for place, ref in enumerate((k_ref, v_ref, q_ref)):
            out_ref[owner, place] = ref[:, start : start + PAIR]


def pack(owners, q, k, v):
    count = q.shape[0]
    return pl.pallas_call(
        lambda *refs: pack_kernel(owners, *refs),
        out_shape=jax.ShapeDtypeStruct((owners, 3, count, PAIR), q.dtype),
    )(q, k, v)


def attend_kernel(got_ref, out_ref, k_ref, va_ref, vc_ref):
    owners, _, count, _ = got_ref.shape
    first = lax.broadcasted_iota(jnp.int32, (count, PAIR), 1) < HEAD_DIM
    one = jnp.ones((count, PAIR), k_ref.dtype)
    zero = jnp.zeros((count, PAIR), k_ref.dtype)
    for s in range(owners):
        rows = pl.ds(s * count, count)
        k_ref[rows, :] = got_ref[s, 0]
        v = got_ref[s, 1]
        va_ref[rows, :] = jnp.where(first, v, one)
        vc_ref[rows, :] = jnp.where(first, one, v)
    keys = k_ref[...]
    factor = HEAD_DIM**-0.5 * LOG2E

    def mixed(queries, values):
        scores = lax.dot_general(
            queries, keys, (((1,), (1,)), ((), ())), preferred_element_type=jnp.float32
        )
        top = jnp.max(scores, axis=-1, keepdims=True)
        expo = jnp.exp2((scores - top) * factor).astype(keys.dtype)
        return jnp.dot(expo, values, preferred_element_type=jnp.float32)

    for s in range(owners):
        q = got_ref[s, 2]
        a = mixed(jnp.where(first, q, zero), va_ref[...])
        c = mixed(jnp.where(first, zero, q), vc_ref[...])
        total = pltpu.roll(jnp.where(first, c, a), HEAD_DIM, 1)
        out_ref[s] = (jnp.where(first, a, c) / total).astype(out_ref.dtype)


def attend(got):
    owners, _, count, _ = got.shape
    rows = owners * count
    return pl.pallas_call(
        attend_kernel,
        out_shape=jax.ShapeDtypeStruct((owners, count, PAIR), got.dtype),
        scratch_shapes=[pltpu.VMEM((rows, PAIR), got.dtype)] * 3,
        compiler_params=pltpu.CompilerParams(vmem_limit_bytes=32 * 1024 * 1024),
    )(got)


def unpack_kernel(back_ref, out_ref):
    owners, count, _ = back_ref.shape
    first = lax.broadcasted_iota(jnp.int32, (count, PAIR), 1) < HEAD_DIM
    for m in range(owners // 4):
        start = 3 * PAIR * m
        middle = jnp.where(first, back_ref[4 * m + 2], back_ref[4 * m + 1])
        out_ref[:, start : start + PAIR] = back_ref[4 * m]
        out_ref[:, start + PAIR : start + 2 * PAIR] = jnp.concatenate(
            [middle[:, HEAD_DIM:], middle[:, :HEAD_DIM]], axis=1
        )
        out_ref[:, start + 2 * PAIR : start + 3 * PAIR] = back_ref[4 * m + 3]


def unpack(back):
    owners, count, _ = back.shape
    return pl.pallas_call(
        unpack_kernel,
        out_shape=jax.ShapeDtypeStruct((count, owners // 4 * 3 * PAIR), back.dtype),
    )(back)


def attend_ring(got, owners):
    size = lax.axis_size("slab")
    _, _, count, _ = got.shape
    rows = owners * count
    tokens = jnp.transpose(got, (1, 0, 2, 3)).reshape(3, rows, 2, HEAD_DIM)
    queries = tokens[2]
    route = [(i, (i + owners) % size) for i in range(size)]

    def absorb(carry, block):
        run_max, run_total, accum = carry
        scores = jnp.einsum("qhd,khd->hqk", queries, block[0], preferred_element_type=jnp.float32)
        scores = scores * HEAD_DIM**-0.5
        new_max = jnp.maximum(run_max, jnp.max(scores, axis=-1))
        shrink = jnp.exp(run_max - new_max)
        expo = jnp.exp(scores - new_max[..., None])
        mix = jnp.einsum(
            "hqk,khd->hqd",
            expo.astype(jnp.bfloat16),
            block[1],
            preferred_element_type=jnp.float32,
        )
        total = run_total * shrink + jnp.sum(expo, axis=-1)
        return new_max, total, accum * shrink[..., None] + mix

    def step(_, pack):
        carry, moving = pack
        moving = lax.ppermute(moving, "slab", route)
        return absorb(carry, moving), moving

    state = (
        jnp.full((2, rows), -1e30, jnp.float32),
        jnp.zeros((2, rows), jnp.float32),
        jnp.zeros((2, rows, HEAD_DIM), jnp.float32),
    )
    state = absorb(state, tokens[:2])
    state, _ = lax.fori_loop(0, size // owners - 1, step, (state, tokens[:2]))
    result = (state[2] / state[1][..., None]).astype(got.dtype)
    return jnp.transpose(result, (1, 0, 2)).reshape(owners, count, PAIR)


def on_device(query_rows, key_rows, value_rows):
    size = lax.axis_size("slab")
    owners = query_rows.shape[1] // TRIPLE * 2
    groups = [list(range(g, g + owners)) for g in range(0, size, owners)]
    exchange = lambda x: lax.all_to_all(x, "slab", 0, 0, axis_index_groups=groups)
    got = exchange(pack(owners, query_rows, key_rows, value_rows))
    result = attend(got) if size == owners else attend_ring(got, owners)
    return unpack(exchange(result))


def solution(mesh):
    spec = P(("batch", "slab"), None)
    return jax.shard_map(
        on_device, mesh=mesh, in_specs=(spec,) * 3, out_specs=spec, check_vma=False
    )
```

```python
import jax
import jax.numpy as jnp
from jax import lax
from jax.experimental import pallas as pl
from jax.experimental.pallas import tpu as pltpu
from jax.sharding import PartitionSpec as P

HEAD_DIM = 64
PAIR = 2 * HEAD_DIM
TRIPLE = 3 * HEAD_DIM
LOG2E = 1.4426950408889634


def window(owner):
    return (owner // 2) * TRIPLE + (owner % 2) * HEAD_DIM


def pack_kernel(owners, q_ref, k_ref, v_ref, out_ref):
    for owner in range(owners):
        start = window(owner)
        for place, ref in enumerate((k_ref, v_ref, q_ref)):
            out_ref[owner, place] = ref[:, start : start + PAIR]


def pack(owners, q, k, v):
    count = q.shape[0]
    return pl.pallas_call(
        lambda *refs: pack_kernel(owners, *refs),
        out_shape=jax.ShapeDtypeStruct((owners, 3, count, PAIR), q.dtype),
        compiler_params=pltpu.CompilerParams(vmem_limit_bytes=8 * 1024 * 1024),
    )(q, k, v)


def attend_kernel(got_ref, out_ref, k_ref, va_ref, vc_ref, qa_ref, qc_ref):
    owners, _, count, _ = got_ref.shape
    first = lax.broadcasted_iota(jnp.int32, (count, PAIR), 1) < HEAD_DIM
    one = jnp.ones((count, PAIR), k_ref.dtype)
    zero = jnp.zeros((count, PAIR), k_ref.dtype)
    for s in range(owners):
        rows = pl.ds(s * count, count)
        k_ref[rows, :] = got_ref[s, 0]
        v = got_ref[s, 1]
        va_ref[rows, :] = jnp.where(first, v, one)
        vc_ref[rows, :] = jnp.where(first, one, v)
        q = got_ref[s, 2]
        qa_ref[rows, :] = jnp.where(first, q, zero)
        qc_ref[rows, :] = jnp.where(first, zero, q)
    factor = HEAD_DIM**-0.5 * LOG2E

    def mixed(q_ref, v_ref):
        scores = lax.dot_general(
            q_ref[...], k_ref[...], (((1,), (1,)), ((), ())), preferred_element_type=jnp.float32
        )
        top = jnp.max(scores, axis=-1, keepdims=True)
        expo = jnp.exp2((scores - top) * factor).astype(k_ref.dtype)
        return jnp.dot(expo, v_ref[...], preferred_element_type=jnp.float32)

    a = mixed(qa_ref, va_ref)
    c = mixed(qc_ref, vc_ref)
    first = lax.broadcasted_iota(jnp.int32, a.shape, 1) < HEAD_DIM
    total = pltpu.roll(jnp.where(first, c, a), HEAD_DIM, 1)
    result = (jnp.where(first, a, c) / total).astype(out_ref.dtype)
    for s in range(owners):
        out_ref[s] = result[s * count : (s + 1) * count]


def attend(got):
    owners, _, count, _ = got.shape
    rows = owners * count
    return pl.pallas_call(
        attend_kernel,
        out_shape=jax.ShapeDtypeStruct((owners, count, PAIR), got.dtype),
        scratch_shapes=[pltpu.VMEM((rows, PAIR), got.dtype)] * 5,
        compiler_params=pltpu.CompilerParams(vmem_limit_bytes=32 * 1024 * 1024),
    )(got)


def unpack_kernel(back_ref, out_ref):
    owners, count, _ = back_ref.shape
    first = lax.broadcasted_iota(jnp.int32, (count, PAIR), 1) < HEAD_DIM
    for m in range(owners // 4):
        start = 3 * PAIR * m
        middle = jnp.where(first, back_ref[4 * m + 2], back_ref[4 * m + 1])
        out_ref[:, start : start + PAIR] = back_ref[4 * m]
        out_ref[:, start + PAIR : start + 2 * PAIR] = jnp.concatenate(
            [middle[:, HEAD_DIM:], middle[:, :HEAD_DIM]], axis=1
        )
        out_ref[:, start + 2 * PAIR : start + 3 * PAIR] = back_ref[4 * m + 3]


def unpack(back):
    owners, count, _ = back.shape
    return pl.pallas_call(
        unpack_kernel,
        out_shape=jax.ShapeDtypeStruct((count, owners // 4 * 3 * PAIR), back.dtype),
        compiler_params=pltpu.CompilerParams(vmem_limit_bytes=8 * 1024 * 1024),
    )(back)


def attend_ring(got, owners):
    size = lax.axis_size("slab")
    _, _, count, _ = got.shape
    rows = owners * count
    tokens = jnp.transpose(got, (1, 0, 2, 3)).reshape(3, rows, 2, HEAD_DIM)
    queries = tokens[2]
    route = [(i, (i + owners) % size) for i in range(size)]

    def absorb(carry, block):
        run_max, run_total, accum = carry
        scores = jnp.einsum("qhd,khd->hqk", queries, block[0], preferred_element_type=jnp.float32)
        scores = scores * HEAD_DIM**-0.5
        new_max = jnp.maximum(run_max, jnp.max(scores, axis=-1))
        shrink = jnp.exp(run_max - new_max)
        expo = jnp.exp(scores - new_max[..., None])
        mix = jnp.einsum(
            "hqk,khd->hqd",
            expo.astype(jnp.bfloat16),
            block[1],
            preferred_element_type=jnp.float32,
        )
        total = run_total * shrink + jnp.sum(expo, axis=-1)
        return new_max, total, accum * shrink[..., None] + mix

    def step(_, pack):
        carry, moving = pack
        moving = lax.ppermute(moving, "slab", route)
        return absorb(carry, moving), moving

    state = (
        jnp.full((2, rows), -1e30, jnp.float32),
        jnp.zeros((2, rows), jnp.float32),
        jnp.zeros((2, rows, HEAD_DIM), jnp.float32),
    )
    state = absorb(state, tokens[:2])
    state, _ = lax.fori_loop(0, size // owners - 1, step, (state, tokens[:2]))
    result = (state[2] / state[1][..., None]).astype(got.dtype)
    return jnp.transpose(result, (1, 0, 2)).reshape(owners, count, PAIR)


def on_device(query_rows, key_rows, value_rows):
    size = lax.axis_size("slab")
    owners = query_rows.shape[1] // TRIPLE * 2
    groups = [list(range(g, g + owners)) for g in range(0, size, owners)]
    exchange = lambda x: lax.all_to_all(x, "slab", 0, 0, axis_index_groups=groups)
    got = exchange(pack(owners, query_rows, key_rows, value_rows))
    result = attend(got) if size == owners else attend_ring(got, owners)
    return unpack(exchange(result))


def solution(mesh):
    spec = P(("batch", "slab"), None)
    return jax.shard_map(
        on_device, mesh=mesh, in_specs=(spec,) * 3, out_specs=spec, check_vma=False
    )
```

```python
import jax
import jax.numpy as jnp
from jax import lax
from jax.experimental import pallas as pl
from jax.experimental.pallas import tpu as pltpu
from jax.sharding import PartitionSpec as P

HEAD_DIM = 64
PAIR = 2 * HEAD_DIM
TRIPLE = 3 * HEAD_DIM
LOG2E = 1.4426950408889634
ROWS = 8


def folds(count):
    part = pl.cdiv(count, 2 * ROWS) * ROWS
    return part, pl.cdiv(count + part, 2 * ROWS) * ROWS


def lanes(shape):
    return lax.broadcasted_iota(jnp.int32, shape, 1) < HEAD_DIM


def swap(x):
    return jnp.concatenate([x[:, HEAD_DIM:], x[:, :HEAD_DIM]], axis=1)


def fold(whole, shared):
    count, part = whole.shape[0], shared.shape[0]
    rows = folds(count)[1]
    rest = [shared, swap(whole[rows:])]
    if part + count - rows < rows:
        rest.append(jnp.zeros((2 * rows - part - count, PAIR), whole.dtype))
    return jnp.where(lanes((rows, PAIR)), whole[:rows], jnp.concatenate(rest, axis=0))


def unfold(block, count):
    part, rows = folds(count)
    return jnp.concatenate([block, swap(block[part : part + count - rows])], axis=0), block[:part]


def pack_kernel(owners, q_hbm, k_hbm, v_hbm, out_ref, q_ref, k_ref, v_ref, sems):
    count = q_ref.shape[0]
    part, rows = folds(count)
    copies = [
        pltpu.make_async_copy(hbm, ref, sems.at[i])
        for i, (hbm, ref) in enumerate(((k_hbm, k_ref), (v_hbm, v_ref), (q_hbm, q_ref)))
    ]
    for copy in copies:
        copy.start()
    first = lanes((count, PAIR))

    def blocks(ref, m):
        left, middle, right = (ref[:, (3 * m + i) * PAIR : (3 * m + i + 1) * PAIR] for i in range(3))
        return left, jnp.where(first, middle, left), swap(jnp.where(first, right, middle)), swap(right)

    for place, (copy, ref) in enumerate(zip(copies, (k_ref, v_ref, q_ref))):
        copy.wait()
        for m in range(owners // 4):
            for i, block in enumerate(blocks(ref, m)):
                if place < 2:
                    out_ref[4 * m + i, place * count : (place + 1) * count] = block
                else:
                    shared = block[:part] if i % 2 == 0 else block[count - part :]
                    out_ref[4 * m + i, 2 * count :] = fold(block, shared)


def pack(owners, q, k, v):
    count = q.shape[0]
    return pl.pallas_call(
        lambda *refs: pack_kernel(owners, *refs),
        out_shape=jax.ShapeDtypeStruct((owners, 2 * count + folds(count)[1], PAIR), q.dtype),
        in_specs=[pl.BlockSpec(memory_space=pltpu.HBM)] * 3,
        scratch_shapes=[pltpu.VMEM(q.shape, q.dtype)] * 3 + [pltpu.SemaphoreType.DMA((3,))],
        compiler_params=pltpu.CompilerParams(vmem_limit_bytes=8 * 1024 * 1024),
    )(q, k, v)


def attend_kernel(count, got_ref, out_ref, k_ref, va_ref, vc_ref, qa_ref, qc_ref):
    owners = got_ref.shape[0]
    part, _ = folds(count)
    first = lanes((count, PAIR))
    one = jnp.ones((count, PAIR), k_ref.dtype)
    zero = jnp.zeros((count, PAIR), k_ref.dtype)
    for s in range(owners):
        rows = pl.ds(s * count, count)
        k_ref[rows, :] = got_ref[s, :count]
        v = got_ref[s, count : 2 * count]
        va_ref[rows, :] = jnp.where(first, v, one)
        vc_ref[rows, :] = jnp.where(first, one, v)
        whole, shared = unfold(got_ref[s, 2 * count :], count)
        qa_ref[rows, :] = jnp.where(first, whole, zero)
        qc_ref[pl.ds(s * part, part), :] = jnp.where(first[:part], zero[:part], shared)
    factor = HEAD_DIM**-0.5 * LOG2E

    def attended(q_ref, v_ref):
        scores = lax.dot_general(
            q_ref[...], k_ref[...], (((1,), (1,)), ((), ())), preferred_element_type=jnp.float32
        )
        top = jnp.max(scores, axis=-1, keepdims=True)
        expo = jnp.exp2((scores - top) * factor).astype(k_ref.dtype)
        mixed = jnp.dot(expo, v_ref[...], preferred_element_type=jnp.float32)
        return (mixed / pltpu.roll(mixed, HEAD_DIM, 1)).astype(out_ref.dtype)

    a = attended(qa_ref, va_ref)
    c = attended(qc_ref, vc_ref)
    for s in range(owners):
        out_ref[s] = fold(a[s * count : (s + 1) * count], c[s * part : (s + 1) * part])


def attend(got, count):
    owners = got.shape[0]
    part, rows = folds(count)
    whole, shared = pltpu.VMEM((owners * count, PAIR), got.dtype), pltpu.VMEM((owners * part, PAIR), got.dtype)
    return pl.pallas_call(
        lambda *refs: attend_kernel(count, *refs),
        out_shape=jax.ShapeDtypeStruct((owners, rows, PAIR), got.dtype),
        scratch_shapes=[whole] * 4 + [shared],
        compiler_params=pltpu.CompilerParams(vmem_limit_bytes=32 * 1024 * 1024),
    )(got)


def unpack_kernel(count, back_ref, out_ref):
    part, _ = folds(count)
    first = lanes((count, PAIR))
    for m in range(back_ref.shape[0] // 4):
        (a, ca), (b, cb), (d, cd), (e, ce) = (
            unfold(back_ref[4 * m + i], count) for i in range(4)
        )
        repeated = 2 * part - count
        tiles = (
            jnp.where(first, a, jnp.concatenate([ca, cb[repeated:]], axis=0)),
            jnp.where(first, b, swap(d)),
            swap(jnp.where(first, e, jnp.concatenate([cd, ce[repeated:]], axis=0))),
        )
        for i, tile in enumerate(tiles):
            out_ref[:, (3 * m + i) * PAIR : (3 * m + i + 1) * PAIR] = tile


def unpack(back, count):
    owners = back.shape[0]
    return pl.pallas_call(
        lambda *refs: unpack_kernel(count, *refs),
        out_shape=jax.ShapeDtypeStruct((count, owners // 4 * 3 * PAIR), back.dtype),
        compiler_params=pltpu.CompilerParams(vmem_limit_bytes=8 * 1024 * 1024),
    )(back)


def attend_ring(got, count):
    owners = got.shape[0]
    size = lax.axis_size("slab")
    part, rows = folds(count)
    split = lambda x: x.reshape(-1, 2, HEAD_DIM)
    own = jnp.stack([split(got[:, :count]), split(got[:, count : 2 * count])])
    whole, shared = jax.vmap(lambda block: unfold(block, count))(got[:, 2 * count :])
    queries = split(whole)[:, 0], split(shared)[:, 1]
    route = [(i, (i + owners) % size) for i in range(size)]

    def absorb(state, block):
        after = []
        for head, (q, (run_max, run_total, accum)) in enumerate(zip(queries, state)):
            scores = jnp.dot(q, block[0, :, head].T, preferred_element_type=jnp.float32) * HEAD_DIM**-0.5
            new_max = jnp.maximum(run_max, jnp.max(scores, axis=-1, keepdims=True))
            shrink = jnp.exp(run_max - new_max)
            expo = jnp.exp(scores - new_max)
            total = run_total * shrink + jnp.sum(expo, axis=-1, keepdims=True)
            mixed = jnp.dot(
                expo.astype(block.dtype), block[1, :, head], preferred_element_type=jnp.float32
            )
            after.append((new_max, total, accum * shrink + mixed))
        return tuple(after)

    def step(_, carry):
        state, moving = carry
        moving = lax.ppermute(moving, "slab", route)
        return absorb(state, moving), moving

    state = tuple(
        (
            jnp.full((q.shape[0], 1), -1e30, jnp.float32),
            jnp.zeros((q.shape[0], 1), jnp.float32),
            jnp.zeros(q.shape, jnp.float32),
        )
        for q in queries
    )
    state, _ = lax.fori_loop(0, size // owners - 1, step, (absorb(state, own), own))
    a, c = ((accum / total).astype(got.dtype) for _, total, accum in state)
    a, c = jnp.pad(a, ((0, 0), (0, HEAD_DIM))), jnp.pad(c, ((0, 0), (HEAD_DIM, 0)))
    return jax.vmap(fold)(a.reshape(owners, count, PAIR), c.reshape(owners, part, PAIR))


def on_device(query_rows, key_rows, value_rows):
    size = lax.axis_size("slab")
    count = query_rows.shape[0]
    owners = query_rows.shape[1] // TRIPLE * 2
    groups = [[g + i for i in members(owners)] for g in range(0, size, owners)]

    def exchange(blocks):
        return lax.all_to_all(blocks, "slab", 0, 0, axis_index_groups=groups)

    got = exchange(pack(owners, query_rows, key_rows, value_rows))
    result = attend(got, count) if size == owners else attend_ring(got, count)
    return unpack(exchange(result), count)


def members(owners):
    start = 5 * owners // 8
    return [(start + i) % owners for i in range(owners)]


def solution(mesh):
    spec = P(("batch", "slab"), None)
    return jax.shard_map(
        on_device, mesh=mesh, in_specs=(spec,) * 3, out_specs=spec, check_vma=False
    )
```

```python
import jax
import jax.numpy as jnp
from jax import lax
from jax.experimental import pallas as pl
from jax.experimental.pallas import tpu as pltpu
from jax.sharding import PartitionSpec as P

HEAD_DIM = 64
PAIR = 2 * HEAD_DIM
TRIPLE = 3 * HEAD_DIM
LOG2E = 1.4426950408889634
ROWS = 8


def folds(count):
    part = pl.cdiv(count, 2 * ROWS) * ROWS
    return part, pl.cdiv(count + part, 2 * ROWS) * ROWS


def lanes(shape):
    return lax.broadcasted_iota(jnp.int32, shape, 1) < HEAD_DIM


def swap(x):
    return jnp.concatenate([x[:, HEAD_DIM:], x[:, :HEAD_DIM]], axis=1)


def fold(whole, shared):
    count, part = whole.shape[0], shared.shape[0]
    rows = folds(count)[1]
    rest = [shared, swap(whole[rows:])]
    if part + count - rows < rows:
        rest.append(jnp.zeros((2 * rows - part - count, PAIR), whole.dtype))
    return jnp.where(lanes((rows, PAIR)), whole[:rows], jnp.concatenate(rest, axis=0))


def unfold(block, count):
    part, rows = folds(count)
    return jnp.concatenate([block, swap(block[part : part + count - rows])], axis=0), block[:part]


def pack_kernel(owners, q_hbm, k_hbm, v_hbm, out_ref, q_ref, k_ref, v_ref, sems):
    count = q_ref.shape[0]
    part, rows = folds(count)
    copies = [
        pltpu.make_async_copy(hbm, ref, sems.at[i])
        for i, (hbm, ref) in enumerate(((k_hbm, k_ref), (v_hbm, v_ref), (q_hbm, q_ref)))
    ]
    for copy in copies:
        copy.start()
    first = lanes((count, PAIR))

    def blocks(ref, m):
        left, middle, right = (ref[:, (3 * m + i) * PAIR : (3 * m + i + 1) * PAIR] for i in range(3))
        return left, jnp.where(first, middle, left), swap(jnp.where(first, right, middle)), swap(right)

    for place, (copy, ref) in enumerate(zip(copies, (k_ref, v_ref, q_ref))):
        copy.wait()
        for m in range(owners // 4):
            for i, block in enumerate(blocks(ref, m)):
                if place < 2:
                    out_ref[4 * m + i, place * count : (place + 1) * count] = block
                else:
                    shared = block[:part] if i % 2 == 0 else block[count - part :]
                    out_ref[4 * m + i, 2 * count :] = fold(block, shared)


def pack(owners, *arrays):
    q, k, v = (pltpu.with_memory_space_constraint(x, pltpu.HBM) for x in arrays)
    count = q.shape[0]
    return pl.pallas_call(
        lambda *refs: pack_kernel(owners, *refs),
        out_shape=jax.ShapeDtypeStruct((owners, 2 * count + folds(count)[1], PAIR), q.dtype),
        in_specs=[pl.BlockSpec(memory_space=pltpu.HBM)] * 3,
        scratch_shapes=[pltpu.VMEM(q.shape, q.dtype)] * 3 + [pltpu.SemaphoreType.DMA((3,))],
        compiler_params=pltpu.CompilerParams(vmem_limit_bytes=8 * 1024 * 1024),
    )(q, k, v)


def attend_kernel(count, got_ref, out_ref, k_ref, va_ref, vc_ref, qa_ref, qc_ref):
    owners = got_ref.shape[0]
    part, _ = folds(count)
    first = lanes((count, PAIR))
    one = jnp.ones((count, PAIR), k_ref.dtype)
    zero = jnp.zeros((count, PAIR), k_ref.dtype)
    for s in range(owners):
        rows = pl.ds(s * count, count)
        k_ref[rows, :] = got_ref[s, :count]
        v = got_ref[s, count : 2 * count]
        va_ref[rows, :] = jnp.where(first, v, one)
        vc_ref[rows, :] = jnp.where(first, one, v)
        whole, shared = unfold(got_ref[s, 2 * count :], count)
        qa_ref[rows, :] = jnp.where(first, whole, zero)
        qc_ref[pl.ds(s * part, part), :] = jnp.where(first[:part], zero[:part], shared)
    factor = HEAD_DIM**-0.5 * LOG2E

    def attended(q_ref, v_ref):
        scores = lax.dot_general(
            q_ref[...], k_ref[...], (((1,), (1,)), ((), ())), preferred_element_type=jnp.float32
        )
        top = jnp.max(scores, axis=-1, keepdims=True)
        expo = jnp.exp2((scores - top) * factor).astype(k_ref.dtype)
        mixed = jnp.dot(expo, v_ref[...], preferred_element_type=jnp.float32)
        return (mixed / pltpu.roll(mixed, HEAD_DIM, 1)).astype(out_ref.dtype)

    a = attended(qa_ref, va_ref)
    c = attended(qc_ref, vc_ref)
    for s in range(owners):
        out_ref[s] = fold(a[s * count : (s + 1) * count], c[s * part : (s + 1) * part])


def attend(got, count):
    owners = got.shape[0]
    part, rows = folds(count)
    whole, shared = pltpu.VMEM((owners * count, PAIR), got.dtype), pltpu.VMEM((owners * part, PAIR), got.dtype)
    return pl.pallas_call(
        lambda *refs: attend_kernel(count, *refs),
        out_shape=jax.ShapeDtypeStruct((owners, rows, PAIR), got.dtype),
        scratch_shapes=[whole] * 4 + [shared],
        compiler_params=pltpu.CompilerParams(vmem_limit_bytes=32 * 1024 * 1024),
    )(got)


def unpack_kernel(count, back_ref, out_ref):
    part, _ = folds(count)
    first = lanes((count, PAIR))
    for m in range(back_ref.shape[0] // 4):
        (a, ca), (b, cb), (d, cd), (e, ce) = (
            unfold(back_ref[4 * m + i], count) for i in range(4)
        )
        repeated = 2 * part - count
        tiles = (
            jnp.where(first, a, jnp.concatenate([ca, cb[repeated:]], axis=0)),
            jnp.where(first, b, swap(d)),
            swap(jnp.where(first, e, jnp.concatenate([cd, ce[repeated:]], axis=0))),
        )
        for i, tile in enumerate(tiles):
            out_ref[:, (3 * m + i) * PAIR : (3 * m + i + 1) * PAIR] = tile


def unpack(back, count):
    owners = back.shape[0]
    return pl.pallas_call(
        lambda *refs: unpack_kernel(count, *refs),
        out_shape=jax.ShapeDtypeStruct((count, owners // 4 * 3 * PAIR), back.dtype),
        compiler_params=pltpu.CompilerParams(vmem_limit_bytes=8 * 1024 * 1024),
    )(back)


def attend_ring(got, count):
    owners = got.shape[0]
    size = lax.axis_size("slab")
    part, rows = folds(count)
    split = lambda x: x.reshape(-1, 2, HEAD_DIM)
    own = jnp.stack([split(got[:, :count]), split(got[:, count : 2 * count])])
    whole, shared = jax.vmap(lambda block: unfold(block, count))(got[:, 2 * count :])
    queries = split(whole)[:, 0], split(shared)[:, 1]
    route = [(i, (i + owners) % size) for i in range(size)]

    def absorb(state, block):
        after = []
        for head, (q, (run_max, run_total, accum)) in enumerate(zip(queries, state)):
            scores = jnp.dot(q, block[0, :, head].T, preferred_element_type=jnp.float32) * HEAD_DIM**-0.5
            new_max = jnp.maximum(run_max, jnp.max(scores, axis=-1, keepdims=True))
            shrink = jnp.exp(run_max - new_max)
            expo = jnp.exp(scores - new_max)
            total = run_total * shrink + jnp.sum(expo, axis=-1, keepdims=True)
            mixed = jnp.dot(
                expo.astype(block.dtype), block[1, :, head], preferred_element_type=jnp.float32
            )
            after.append((new_max, total, accum * shrink + mixed))
        return tuple(after)

    def step(_, carry):
        state, moving = carry
        moving = lax.ppermute(moving, "slab", route)
        return absorb(state, moving), moving

    state = tuple(
        (
            jnp.full((q.shape[0], 1), -1e30, jnp.float32),
            jnp.zeros((q.shape[0], 1), jnp.float32),
            jnp.zeros(q.shape, jnp.float32),
        )
        for q in queries
    )
    state, _ = lax.fori_loop(0, size // owners - 1, step, (absorb(state, own), own))
    a, c = ((accum / total).astype(got.dtype) for _, total, accum in state)
    a, c = jnp.pad(a, ((0, 0), (0, HEAD_DIM))), jnp.pad(c, ((0, 0), (HEAD_DIM, 0)))
    return jax.vmap(fold)(a.reshape(owners, count, PAIR), c.reshape(owners, part, PAIR))


def on_device(query_rows, key_rows, value_rows):
    size = lax.axis_size("slab")
    count = query_rows.shape[0]
    owners = query_rows.shape[1] // TRIPLE * 2
    groups = [[g + i for i in members(owners)] for g in range(0, size, owners)]

    def exchange(blocks):
        return lax.all_to_all(blocks, "slab", 0, 0, axis_index_groups=groups)

    got = exchange(pack(owners, query_rows, key_rows, value_rows))
    result = attend(got, count) if size == owners else attend_ring(got, count)
    return unpack(exchange(result), count)


def members(owners):
    start = 5 * owners // 8
    return [(start + i) % owners for i in range(owners)]


def solution(mesh):
    spec = P(("batch", "slab"), None)
    return jax.shard_map(
        on_device, mesh=mesh, in_specs=(spec,) * 3, out_specs=spec, check_vma=False
    )
```

```python
import jax
import jax.numpy as jnp
from jax import lax
from jax.experimental import pallas as pl
from jax.experimental.pallas import tpu as pltpu
from jax.sharding import PartitionSpec as P

HEAD_DIM = 64
PAIR = 2 * HEAD_DIM
TRIPLE = 3 * HEAD_DIM
LOG2E = 1.4426950408889634
ROWS = 8


def folds(count):
    part = pl.cdiv(count, 2 * ROWS) * ROWS
    return part, pl.cdiv(count + part, 2 * ROWS) * ROWS


def lanes(shape):
    return lax.broadcasted_iota(jnp.int32, shape, 1) < HEAD_DIM


def swap(x):
    return jnp.concatenate([x[:, HEAD_DIM:], x[:, :HEAD_DIM]], axis=1)


def fold(whole, shared):
    count, part = whole.shape[0], shared.shape[0]
    rows = folds(count)[1]
    rest = [shared, swap(whole[rows:])]
    if part + count - rows < rows:
        rest.append(jnp.zeros((2 * rows - part - count, PAIR), whole.dtype))
    return jnp.where(lanes((rows, PAIR)), whole[:rows], jnp.concatenate(rest, axis=0))


def unfold(block, count):
    part, rows = folds(count)
    return jnp.concatenate([block, swap(block[part : part + count - rows])], axis=0), block[:part]


def pack_kernel(owners, q_hbm, k_hbm, v_hbm, out_ref, q_ref, k_ref, v_ref, sems):
    count = q_ref.shape[0]
    part, rows = folds(count)
    copies = [
        pltpu.make_async_copy(hbm, ref, sems.at[i])
        for i, (hbm, ref) in enumerate(((k_hbm, k_ref), (v_hbm, v_ref), (q_hbm, q_ref)))
    ]
    for copy in copies:
        copy.start()
    first = lanes((count, PAIR))

    def blocks(ref, m):
        left, middle, right = (ref[:, (3 * m + i) * PAIR : (3 * m + i + 1) * PAIR] for i in range(3))
        return left, jnp.where(first, middle, left), swap(jnp.where(first, right, middle)), swap(right)

    for place, (copy, ref) in enumerate(zip(copies, (k_ref, v_ref, q_ref))):
        copy.wait()
        for m in range(owners // 4):
            for i, block in enumerate(blocks(ref, m)):
                if place < 2:
                    out_ref[4 * m + i, place * count : (place + 1) * count] = block
                else:
                    shared = block[:part] if i % 2 == 0 else block[count - part :]
                    out_ref[4 * m + i, 2 * count :] = fold(block, shared)


def pack(owners, *arrays):
    q, k, v = (pltpu.with_memory_space_constraint(x, pltpu.HBM) for x in arrays)
    count = q.shape[0]
    return pl.pallas_call(
        lambda *refs: pack_kernel(owners, *refs),
        out_shape=jax.ShapeDtypeStruct((owners, 2 * count + folds(count)[1], PAIR), q.dtype),
        in_specs=[pl.BlockSpec(memory_space=pltpu.HBM)] * 3,
        scratch_shapes=[pltpu.VMEM(q.shape, q.dtype)] * 3 + [pltpu.SemaphoreType.DMA((3,))],
        compiler_params=pltpu.CompilerParams(vmem_limit_bytes=8 * 1024 * 1024),
    )(q, k, v)


def attend_kernel(count, got_ref, out_ref, k_ref, va_ref, vc_ref, qa_ref, qc_ref):
    owners = got_ref.shape[0]
    part, _ = folds(count)
    first = lanes((count, PAIR))
    one = jnp.ones((count, PAIR), k_ref.dtype)
    zero = jnp.zeros((count, PAIR), k_ref.dtype)
    for s in range(owners):
        rows = pl.ds(s * count, count)
        k_ref[rows, :] = got_ref[s, :count]
        v = got_ref[s, count : 2 * count]
        va_ref[rows, :] = jnp.where(first, v, one)
        vc_ref[rows, :] = jnp.where(first, one, v)
        whole, shared = unfold(got_ref[s, 2 * count :], count)
        qa_ref[rows, :] = jnp.where(first, whole, zero)
        qc_ref[pl.ds(s * part, part), :] = jnp.where(first[:part], zero[:part], shared)
    factor = HEAD_DIM**-0.5 * LOG2E

    def score(q_ref, rows):
        return lax.dot_general(
            q_ref[rows, :], k_ref[...], (((1,), (1,)), ((), ())), preferred_element_type=jnp.float32
        )

    def weigh(scores):
        top = jnp.max(scores, axis=-1, keepdims=True)
        return jnp.exp2((scores - top) * factor).astype(k_ref.dtype)

    def mix(weights, v_ref):
        mixed = jnp.dot(weights, v_ref[...], preferred_element_type=jnp.float32)
        return (mixed / pltpu.roll(mixed, HEAD_DIM, 1)).astype(out_ref.dtype)

    half = owners // 2 * count
    parts = (
        (qa_ref, pl.ds(0, half), va_ref),
        (qa_ref, pl.ds(half, half), va_ref),
        (qc_ref, slice(None), vc_ref),
    )
    held, results = [], []
    for step in range(len(parts) + 2):
        if step < len(parts):
            held.append(score(*parts[step][:2]))
        if 1 <= step <= len(parts):
            held[step - 1] = weigh(held[step - 1])
        if step >= 2:
            results.append(mix(held[step - 2], parts[step - 2][2]))
    a, c = jnp.concatenate(results[:2], axis=0), results[2]
    for s in range(owners):
        out_ref[s] = fold(a[s * count : (s + 1) * count], c[s * part : (s + 1) * part])


def attend(got, count):
    owners = got.shape[0]
    part, rows = folds(count)
    whole, shared = pltpu.VMEM((owners * count, PAIR), got.dtype), pltpu.VMEM((owners * part, PAIR), got.dtype)
    return pl.pallas_call(
        lambda *refs: attend_kernel(count, *refs),
        out_shape=jax.ShapeDtypeStruct((owners, rows, PAIR), got.dtype),
        scratch_shapes=[whole] * 4 + [shared],
        compiler_params=pltpu.CompilerParams(vmem_limit_bytes=32 * 1024 * 1024),
    )(got)


def unpack_kernel(count, back_ref, out_ref):
    part, _ = folds(count)
    first = lanes((count, PAIR))
    for m in range(back_ref.shape[0] // 4):
        (a, ca), (b, cb), (d, cd), (e, ce) = (
            unfold(back_ref[4 * m + i], count) for i in range(4)
        )
        repeated = 2 * part - count
        tiles = (
            jnp.where(first, a, jnp.concatenate([ca, cb[repeated:]], axis=0)),
            jnp.where(first, b, swap(d)),
            swap(jnp.where(first, e, jnp.concatenate([cd, ce[repeated:]], axis=0))),
        )
        for i, tile in enumerate(tiles):
            out_ref[:, (3 * m + i) * PAIR : (3 * m + i + 1) * PAIR] = tile


def unpack(back, count):
    owners = back.shape[0]
    return pl.pallas_call(
        lambda *refs: unpack_kernel(count, *refs),
        out_shape=jax.ShapeDtypeStruct((count, owners // 4 * 3 * PAIR), back.dtype),
        compiler_params=pltpu.CompilerParams(vmem_limit_bytes=8 * 1024 * 1024),
    )(back)


def attend_ring(got, count):
    owners = got.shape[0]
    size = lax.axis_size("slab")
    part, rows = folds(count)
    split = lambda x: x.reshape(-1, 2, HEAD_DIM)
    own = jnp.stack([split(got[:, :count]), split(got[:, count : 2 * count])])
    whole, shared = jax.vmap(lambda block: unfold(block, count))(got[:, 2 * count :])
    queries = split(whole)[:, 0], split(shared)[:, 1]
    route = [(i, (i + owners) % size) for i in range(size)]

    def absorb(state, block):
        after = []
        for head, (q, (run_max, run_total, accum)) in enumerate(zip(queries, state)):
            scores = jnp.dot(q, block[0, :, head].T, preferred_element_type=jnp.float32) * HEAD_DIM**-0.5
            new_max = jnp.maximum(run_max, jnp.max(scores, axis=-1, keepdims=True))
            shrink = jnp.exp(run_max - new_max)
            expo = jnp.exp(scores - new_max)
            total = run_total * shrink + jnp.sum(expo, axis=-1, keepdims=True)
            mixed = jnp.dot(
                expo.astype(block.dtype), block[1, :, head], preferred_element_type=jnp.float32
            )
            after.append((new_max, total, accum * shrink + mixed))
        return tuple(after)

    def step(_, carry):
        state, moving = carry
        moving = lax.ppermute(moving, "slab", route)
        return absorb(state, moving), moving

    state = tuple(
        (
            jnp.full((q.shape[0], 1), -1e30, jnp.float32),
            jnp.zeros((q.shape[0], 1), jnp.float32),
            jnp.zeros(q.shape, jnp.float32),
        )
        for q in queries
    )
    state, _ = lax.fori_loop(0, size // owners - 1, step, (absorb(state, own), own))
    a, c = ((accum / total).astype(got.dtype) for _, total, accum in state)
    a, c = jnp.pad(a, ((0, 0), (0, HEAD_DIM))), jnp.pad(c, ((0, 0), (HEAD_DIM, 0)))
    return jax.vmap(fold)(a.reshape(owners, count, PAIR), c.reshape(owners, part, PAIR))


def on_device(query_rows, key_rows, value_rows):
    size = lax.axis_size("slab")
    count = query_rows.shape[0]
    owners = query_rows.shape[1] // TRIPLE * 2
    groups = [[g + i for i in members(owners)] for g in range(0, size, owners)]

    def exchange(blocks):
        return lax.all_to_all(blocks, "slab", 0, 0, axis_index_groups=groups)

    got = exchange(pack(owners, query_rows, key_rows, value_rows))
    result = attend(got, count) if size == owners else attend_ring(got, count)
    return unpack(exchange(result), count)


def members(owners):
    start = 5 * owners // 8
    return [(start + i) % owners for i in range(owners)]


def solution(mesh):
    spec = P(("batch", "slab"), None)
    return jax.shard_map(
        on_device, mesh=mesh, in_specs=(spec,) * 3, out_specs=spec, check_vma=False
    )
```

```python
import jax
import jax.numpy as jnp
from jax import lax
from jax.experimental import pallas as pl
from jax.experimental.pallas import tpu as pltpu
from jax.sharding import PartitionSpec as P

HEAD_DIM = 64
PAIR = 2 * HEAD_DIM
TRIPLE = 3 * HEAD_DIM
LOG2E = 1.4426950408889634
ROWS = 8


def folds(count):
    part = pl.cdiv(count, 2 * ROWS) * ROWS
    return part, pl.cdiv(count + part, 2 * ROWS) * ROWS


def lanes(shape):
    return lax.broadcasted_iota(jnp.int32, shape, 1) < HEAD_DIM


def swap(x):
    return jnp.concatenate([x[:, HEAD_DIM:], x[:, :HEAD_DIM]], axis=1)


def fold(whole, shared):
    count, part = whole.shape[0], shared.shape[0]
    rows = folds(count)[1]
    rest = [shared, swap(whole[rows:])]
    if part + count - rows < rows:
        rest.append(jnp.zeros((2 * rows - part - count, PAIR), whole.dtype))
    return jnp.where(lanes((rows, PAIR)), whole[:rows], jnp.concatenate(rest, axis=0))


def unfold(block, count):
    part, rows = folds(count)
    return jnp.concatenate([block, swap(block[part : part + count - rows])], axis=0), block[:part]


def pack_kernel(owners, q_hbm, k_hbm, v_hbm, out_ref, q_ref, k_ref, v_ref, sems):
    count = q_ref.shape[0]
    part, rows = folds(count)
    copies = [
        pltpu.make_async_copy(hbm, ref, sems.at[i])
        for i, (hbm, ref) in enumerate(((k_hbm, k_ref), (v_hbm, v_ref), (q_hbm, q_ref)))
    ]
    for copy in copies:
        copy.start()
    first = lanes((count, PAIR))

    def blocks(ref, m):
        left, middle, right = (ref[:, (3 * m + i) * PAIR : (3 * m + i + 1) * PAIR] for i in range(3))
        return left, jnp.where(first, middle, left), swap(jnp.where(first, right, middle)), swap(right)

    for place, (copy, ref) in enumerate(zip(copies, (k_ref, v_ref, q_ref))):
        copy.wait()
        for m in range(owners // 4):
            for i, block in enumerate(blocks(ref, m)):
                if place < 2:
                    out_ref[4 * m + i, place * count : (place + 1) * count] = block
                else:
                    shared = block[:part] if i % 2 == 0 else block[count - part :]
                    out_ref[4 * m + i, 2 * count :] = fold(block, shared)


def pack(owners, *arrays):
    q, k, v = (pltpu.with_memory_space_constraint(x, pltpu.HBM) for x in arrays)
    count = q.shape[0]
    return pl.pallas_call(
        lambda *refs: pack_kernel(owners, *refs),
        out_shape=jax.ShapeDtypeStruct((owners, 2 * count + folds(count)[1], PAIR), q.dtype),
        in_specs=[pl.BlockSpec(memory_space=pltpu.HBM)] * 3,
        scratch_shapes=[pltpu.VMEM(q.shape, q.dtype)] * 3 + [pltpu.SemaphoreType.DMA((3,))],
        compiler_params=pltpu.CompilerParams(vmem_limit_bytes=8 * 1024 * 1024),
    )(q, k, v)


def attend_kernel(count, got_ref, out_ref, k_ref, va_ref, vc_ref, qa_ref, qc_ref):
    owners = got_ref.shape[0]
    part, _ = folds(count)
    first = lanes((count, PAIR))
    one = jnp.ones((count, PAIR), k_ref.dtype)
    zero = jnp.zeros((count, PAIR), k_ref.dtype)
    for s in range(owners):
        rows = pl.ds(s * count, count)
        k_ref[rows, :] = got_ref[s, :count]
        v = got_ref[s, count : 2 * count]
        va_ref[rows, :] = jnp.where(first, v, one)
        vc_ref[rows, :] = jnp.where(first, one, v)
        whole, shared = unfold(got_ref[s, 2 * count :], count)
        qa_ref[rows, :] = jnp.where(first, whole, zero)
        qc_ref[pl.ds(s * part, part), :] = jnp.where(first[:part], zero[:part], shared)
    factor = HEAD_DIM**-0.5 * LOG2E

    def score(q_ref, rows):
        return lax.dot_general(
            q_ref[rows, :], k_ref[...], (((1,), (1,)), ((), ())), preferred_element_type=jnp.float32
        )

    def weigh(scores):
        top = jnp.max(scores, axis=-1, keepdims=True)
        return jnp.exp2((scores - top) * factor).astype(k_ref.dtype)

    def mix(weights, v_ref):
        mixed = jnp.dot(weights, v_ref[...], preferred_element_type=jnp.float32)
        return (mixed / pltpu.roll(mixed, HEAD_DIM, 1)).astype(out_ref.dtype)

    half = owners // 2 * count
    parts = (
        (qa_ref, pl.ds(0, half), va_ref),
        (qa_ref, pl.ds(half, half), va_ref),
        (qc_ref, slice(None), vc_ref),
    )
    held, results = [], []
    for step in range(len(parts) + 2):
        if step < len(parts):
            held.append(score(*parts[step][:2]))
        if 1 <= step <= len(parts):
            held[step - 1] = weigh(held[step - 1])
        if step >= 2:
            results.append(mix(held[step - 2], parts[step - 2][2]))
    a, c = jnp.concatenate(results[:2], axis=0), results[2]
    for s in range(owners):
        out_ref[s] = fold(a[s * count : (s + 1) * count], c[s * part : (s + 1) * part])


def attend(got, count):
    owners = got.shape[0]
    part, rows = folds(count)
    whole, shared = pltpu.VMEM((owners * count, PAIR), got.dtype), pltpu.VMEM((owners * part, PAIR), got.dtype)
    return pl.pallas_call(
        lambda *refs: attend_kernel(count, *refs),
        out_shape=jax.ShapeDtypeStruct((owners, rows, PAIR), got.dtype),
        scratch_shapes=[whole] * 4 + [shared],
        compiler_params=pltpu.CompilerParams(vmem_limit_bytes=32 * 1024 * 1024),
    )(got)


def unpack_kernel(count, back_ref, out_ref):
    part, _ = folds(count)
    first = lanes((count, PAIR))
    for m in range(back_ref.shape[0] // 4):
        (a, ca), (b, cb), (d, cd), (e, ce) = (
            unfold(back_ref[4 * m + i], count) for i in range(4)
        )
        repeated = 2 * part - count
        tiles = (
            jnp.where(first, a, jnp.concatenate([ca, cb[repeated:]], axis=0)),
            jnp.where(first, b, swap(d)),
            swap(jnp.where(first, e, jnp.concatenate([cd, ce[repeated:]], axis=0))),
        )
        for i, tile in enumerate(tiles):
            out_ref[:, (3 * m + i) * PAIR : (3 * m + i + 1) * PAIR] = tile


def unpack(back, count):
    owners = back.shape[0]
    return pl.pallas_call(
        lambda *refs: unpack_kernel(count, *refs),
        out_shape=jax.ShapeDtypeStruct((count, owners // 4 * 3 * PAIR), back.dtype),
        compiler_params=pltpu.CompilerParams(vmem_limit_bytes=8 * 1024 * 1024),
    )(back)


def attend_ring(got, count):
    owners = got.shape[0]
    size = lax.axis_size("slab")
    part, rows = folds(count)
    split = lambda x: x.reshape(-1, 2, HEAD_DIM)
    own = jnp.stack([split(got[:, :count]), split(got[:, count : 2 * count])])
    whole, shared = jax.vmap(lambda block: unfold(block, count))(got[:, 2 * count :])
    queries = split(whole)[:, 0], split(shared)[:, 1]
    route = [(i, (i + owners) % size) for i in range(size)]

    def absorb(state, block):
        after = []
        for head, (q, (run_max, run_total, accum)) in enumerate(zip(queries, state)):
            scores = jnp.dot(q, block[0, :, head].T, preferred_element_type=jnp.float32) * HEAD_DIM**-0.5
            new_max = jnp.maximum(run_max, jnp.max(scores, axis=-1, keepdims=True))
            shrink = jnp.exp(run_max - new_max)
            expo = jnp.exp(scores - new_max)
            total = run_total * shrink + jnp.sum(expo, axis=-1, keepdims=True)
            mixed = jnp.dot(
                expo.astype(block.dtype), block[1, :, head], preferred_element_type=jnp.float32
            )
            after.append((new_max, total, accum * shrink + mixed))
        return tuple(after)

    def step(_, carry):
        state, moving = carry
        moving = lax.ppermute(moving, "slab", route)
        return absorb(state, moving), moving

    state = tuple(
        (
            jnp.full((q.shape[0], 1), -1e30, jnp.float32),
            jnp.zeros((q.shape[0], 1), jnp.float32),
            jnp.zeros(q.shape, jnp.float32),
        )
        for q in queries
    )
    state, _ = lax.fori_loop(0, size // owners - 1, step, (absorb(state, own), own))
    a, c = ((accum / total).astype(got.dtype) for _, total, accum in state)
    a, c = jnp.pad(a, ((0, 0), (0, HEAD_DIM))), jnp.pad(c, ((0, 0), (HEAD_DIM, 0)))
    return jax.vmap(fold)(a.reshape(owners, count, PAIR), c.reshape(owners, part, PAIR))


def on_device(query_rows, key_rows, value_rows):
    size = lax.axis_size("slab")
    count = query_rows.shape[0]
    owners = query_rows.shape[1] // TRIPLE * 2
    groups = [[g + i for i in members(owners)] for g in range(0, size, owners)]

    def exchange(blocks):
        return lax.all_to_all(blocks, "slab", 0, 0, axis_index_groups=groups)

    got = exchange(pack(owners, query_rows, key_rows, value_rows))
    result = attend(got, count) if size == owners else attend_ring(got, count)
    return unpack(exchange(result), count)


def members(owners):
    middle = 5 * owners // 8
    return [middle] + [i ^ 1 for i in range(owners) if i ^ 1 != middle]


def solution(mesh):
    spec = P(("batch", "slab"), None)
    return jax.shard_map(
        on_device, mesh=mesh, in_specs=(spec,) * 3, out_specs=spec, check_vma=False
    )
```

```python
import jax
import jax.numpy as jnp
from jax import lax
from jax.experimental import pallas as pl
from jax.experimental.pallas import tpu as pltpu
from jax.sharding import PartitionSpec as P

HEAD_DIM = 64
PAIR = 2 * HEAD_DIM
TRIPLE = 3 * HEAD_DIM
LOG2E = 1.4426950408889634
ROWS = 8


def folds(count):
    part = pl.cdiv(count, 2 * ROWS) * ROWS
    return part, pl.cdiv(count + part, 2 * ROWS) * ROWS


def lanes(shape):
    return lax.broadcasted_iota(jnp.int32, shape, 1) < HEAD_DIM


def swap(x):
    return jnp.concatenate([x[:, HEAD_DIM:], x[:, :HEAD_DIM]], axis=1)


def fold(whole, shared):
    count, part = whole.shape[0], shared.shape[0]
    rows = folds(count)[1]
    rest = [shared, swap(whole[rows:])]
    if part + count - rows < rows:
        rest.append(jnp.zeros((2 * rows - part - count, PAIR), whole.dtype))
    return jnp.where(lanes((rows, PAIR)), whole[:rows], jnp.concatenate(rest, axis=0))


def unfold(block, count):
    part, rows = folds(count)
    return jnp.concatenate([block, swap(block[part : part + count - rows])], axis=0), block[:part]


def pack_kernel(owners, q_hbm, k_hbm, v_hbm, out_ref, q_ref, k_ref, v_ref, sems):
    count = q_ref.shape[0]
    part, rows = folds(count)
    copies = [
        pltpu.make_async_copy(hbm, ref, sems.at[i])
        for i, (hbm, ref) in enumerate(((k_hbm, k_ref), (v_hbm, v_ref), (q_hbm, q_ref)))
    ]
    for copy in copies:
        copy.start()
    first = lanes((count, PAIR))

    def blocks(ref, m):
        left, middle, right = (ref[:, (3 * m + i) * PAIR : (3 * m + i + 1) * PAIR] for i in range(3))
        return left, jnp.where(first, middle, left), swap(jnp.where(first, right, middle)), swap(right)

    for place, (copy, ref) in enumerate(zip(copies, (k_ref, v_ref, q_ref))):
        copy.wait()
        for m in range(owners // 4):
            for i, block in enumerate(blocks(ref, m)):
                if place < 2:
                    out_ref[4 * m + i, place * count : (place + 1) * count] = block
                else:
                    shared = block[:part] if i % 2 == 0 else block[count - part :]
                    out_ref[4 * m + i, 2 * count :] = fold(block, shared)


def pack(owners, *arrays):
    q, k, v = (pltpu.with_memory_space_constraint(x, pltpu.HBM) for x in arrays)
    count = q.shape[0]
    return pl.pallas_call(
        lambda *refs: pack_kernel(owners, *refs),
        out_shape=jax.ShapeDtypeStruct((owners, 2 * count + folds(count)[1], PAIR), q.dtype),
        in_specs=[pl.BlockSpec(memory_space=pltpu.HBM)] * 3,
        scratch_shapes=[pltpu.VMEM(q.shape, q.dtype)] * 3 + [pltpu.SemaphoreType.DMA((3,))],
        compiler_params=pltpu.CompilerParams(vmem_limit_bytes=8 * 1024 * 1024),
    )(q, k, v)


def attend_kernel(count, got_ref, out_ref, k_ref, va_ref, vc_ref, qa_ref, qc_ref):
    owners = got_ref.shape[0]
    part, _ = folds(count)
    first = lanes((count, PAIR))
    one = jnp.ones((count, PAIR), k_ref.dtype)
    zero = jnp.zeros((count, PAIR), k_ref.dtype)
    for s in range(owners):
        rows = pl.ds(s * count, count)
        k_ref[rows, :] = got_ref[s, :count]
        v = got_ref[s, count : 2 * count]
        va_ref[rows, :] = jnp.where(first, v, one)
        vc_ref[rows, :] = jnp.where(first, one, v)
        whole, shared = unfold(got_ref[s, 2 * count :], count)
        qa_ref[rows, :] = jnp.where(first, whole, zero)
        qc_ref[pl.ds(s * part, part), :] = jnp.where(first[:part], zero[:part], shared)
    factor = HEAD_DIM**-0.5 * LOG2E

    def score(q_ref, rows):
        return lax.dot_general(
            q_ref[rows, :], k_ref[...], (((1,), (1,)), ((), ())), preferred_element_type=jnp.float32
        )

    def weigh(scores):
        top = jnp.max(scores, axis=-1, keepdims=True)
        return jnp.exp2((scores - top) * factor).astype(k_ref.dtype)

    def mix(weights, v_ref):
        mixed = jnp.dot(weights, v_ref[...], preferred_element_type=jnp.float32)
        return (mixed / pltpu.roll(mixed, HEAD_DIM, 1)).astype(out_ref.dtype)

    half = owners // 2 * count
    parts = (
        (qa_ref, pl.ds(0, half), va_ref),
        (qa_ref, pl.ds(half, half), va_ref),
        (qc_ref, slice(None), vc_ref),
    )
    held, results = [], []
    for step in range(len(parts) + 2):
        if step < len(parts):
            held.append(score(*parts[step][:2]))
        if 1 <= step <= len(parts):
            held[step - 1] = weigh(held[step - 1])
        if step >= 2:
            results.append(mix(held[step - 2], parts[step - 2][2]))
    a, c = jnp.concatenate(results[:2], axis=0), results[2]
    for s in range(owners):
        out_ref[s] = fold(a[s * count : (s + 1) * count], c[s * part : (s + 1) * part])


def attend(got, count):
    owners = got.shape[0]
    part, rows = folds(count)
    whole, shared = pltpu.VMEM((owners * count, PAIR), got.dtype), pltpu.VMEM((owners * part, PAIR), got.dtype)
    return pl.pallas_call(
        lambda *refs: attend_kernel(count, *refs),
        out_shape=jax.ShapeDtypeStruct((owners, rows, PAIR), got.dtype),
        scratch_shapes=[whole] * 4 + [shared],
        compiler_params=pltpu.CompilerParams(vmem_limit_bytes=32 * 1024 * 1024),
    )(got)


def unpack_kernel(count, back_ref, out_ref):
    part, _ = folds(count)
    first = lanes((count, PAIR))
    for m in range(back_ref.shape[0] // 4):
        (a, ca), (b, cb), (d, cd), (e, ce) = (
            unfold(back_ref[4 * m + i], count) for i in range(4)
        )
        repeated = 2 * part - count
        tiles = (
            jnp.where(first, a, jnp.concatenate([ca, cb[repeated:]], axis=0)),
            jnp.where(first, b, swap(d)),
            swap(jnp.where(first, e, jnp.concatenate([cd, ce[repeated:]], axis=0))),
        )
        for i, tile in enumerate(tiles):
            out_ref[:, (3 * m + i) * PAIR : (3 * m + i + 1) * PAIR] = tile


def unpack(back, count):
    owners = back.shape[0]
    return pl.pallas_call(
        lambda *refs: unpack_kernel(count, *refs),
        out_shape=jax.ShapeDtypeStruct((count, owners // 4 * 3 * PAIR), back.dtype),
        compiler_params=pltpu.CompilerParams(vmem_limit_bytes=8 * 1024 * 1024),
    )(back)


def attend_ring(got, count):
    owners = got.shape[0]
    size = lax.axis_size("slab")
    part, rows = folds(count)
    split = lambda x: x.reshape(-1, 2, HEAD_DIM)
    own = jnp.stack([split(got[:, :count]), split(got[:, count : 2 * count])])
    whole, shared = jax.vmap(lambda block: unfold(block, count))(got[:, 2 * count :])
    queries = split(whole)[:, 0], split(shared)[:, 1]
    route = [(i, (i + owners) % size) for i in range(size)]

    def absorb(state, block):
        after = []
        for head, (q, (run_max, run_total, accum)) in enumerate(zip(queries, state)):
            scores = jnp.dot(q, block[0, :, head].T, preferred_element_type=jnp.float32) * HEAD_DIM**-0.5
            new_max = jnp.maximum(run_max, jnp.max(scores, axis=-1, keepdims=True))
            shrink = jnp.exp(run_max - new_max)
            expo = jnp.exp(scores - new_max)
            total = run_total * shrink + jnp.sum(expo, axis=-1, keepdims=True)
            mixed = jnp.dot(
                expo.astype(block.dtype), block[1, :, head], preferred_element_type=jnp.float32
            )
            after.append((new_max, total, accum * shrink + mixed))
        return tuple(after)

    def step(_, carry):
        state, moving = carry
        moving = lax.ppermute(moving, "slab", route)
        return absorb(state, moving), moving

    state = tuple(
        (
            jnp.full((q.shape[0], 1), -1e30, jnp.float32),
            jnp.zeros((q.shape[0], 1), jnp.float32),
            jnp.zeros(q.shape, jnp.float32),
        )
        for q in queries
    )
    state, _ = lax.fori_loop(0, size // owners - 1, step, (absorb(state, own), own))
    a, c = ((accum / total).astype(got.dtype) for _, total, accum in state)
    a, c = jnp.pad(a, ((0, 0), (0, HEAD_DIM))), jnp.pad(c, ((0, 0), (HEAD_DIM, 0)))
    return jax.vmap(fold)(a.reshape(owners, count, PAIR), c.reshape(owners, part, PAIR))


def on_device(query_rows, key_rows, value_rows):
    size = lax.axis_size("slab")
    count = query_rows.shape[0]
    owners = query_rows.shape[1] // TRIPLE * 2
    groups = [[g + i for i in members(owners)] for g in range(0, size, owners)]

    def exchange(blocks):
        return lax.all_to_all(blocks, "slab", 0, 0, axis_index_groups=groups)

    got = exchange(pack(owners, query_rows, key_rows, value_rows))
    result = attend(got, count) if size == owners else attend_ring(got, count)
    return unpack(exchange(result), count)


def members(owners):
    order = (11, 8, 3, 15, 10, 7, 2, 0, 4, 14, 5, 1, 9, 13, 6, 12)
    return list(order) if len(order) == owners else list(range(owners))


def solution(mesh):
    spec = P(("batch", "slab"), None)
    return jax.shard_map(
        on_device, mesh=mesh, in_specs=(spec,) * 3, out_specs=spec, check_vma=False
    )
```
